32 devices in a mesh: tm: 8 (over z, x), wafer: 4 (over y, core).
Axes of the slice: x: 2, y: 2, z: 4, core: 2. Of those that a mesh axis runs over, the one named last changes fastest.
Arguments:
- timestream: bfloat16 [1024, 32768], P('wafer', 'tm'), may hold values from -6 to 6
- sample_weight: bfloat16 [1024, 32768], P('wafer', 'tm'), may hold values from 0 to 4
- response: float32 [3, 1024], replicated, may hold values from -1 to 1
- band_filter: bfloat16 [256, 256], replicated, may hold values from -0.375 to 0.375
- whiten: bfloat16 [7, 1024, 1024], P(None, ('tm', 'wafer')), as said below
- group_wafer: int32 [8], replicated, may hold values from 0 to 6
- pointing: bfloat16 [128, 6, 256, 256], P(('tm', 'wafer')), may hold values from -0.15625 to 0.15625
- tile_list: int32 [128, 6], P(('tm', 'wafer')), may hold values from 0 to 255, as said below
- tile_home: int32 [256], replicated, may hold values from 0 to 255, as said below
- solution: float32 [256, 3, 256], P('tm'), may hold values from -6 to 6
- direction: float32 [256, 3, 256], P('tm'), may hold values from -6 to 6
- cg_scalars: float32 [2], replicated, may hold values from 0.5 to 1.5
Outputs:
- solution_next: float32 [256, 3, 256], P('tm')
- residual_next: float32 [256, 3, 256], P('tm')
- direction_next: float32 [256, 3, 256], P('tm')
The draws below stay inside these ranges and needn't reach their ends.
Inputs may be any that keep to these rules, and one draw needn't show every extreme that they name: `tile_list`: the tiles named in the spans of one device (one index of tm and one of wafer) are all different; among them at most 3 have their row tile_home on one index of tm, and in every draw, for each index of wafer, some index of tm owns exactly 3 tiles named by every device of that wafer index. A permutation: row tile_home[i] of a map holds sky tile i. `whiten`: each whitening matrix is symmetric.
All inputs are finite; a program needn't handle non-finite values.
Results may differ from the reference program's by a relative error of at most 0.0033.
The reference program's roundings to bfloat16 on the way (of `short_map`, `errors`, `filtered`, `whitened`, `smoothed` and `stokes`) count: a program that leaves them out, or rounds other values in their place, can miss the bound.
Values may be sent and summed in bfloat16 or wider, within the bound.
A program may use at most 128 MiB of HBM per device.

```python
import math
import jax
import jax.numpy as jnp
from jax import lax

WDET = 1024
WAFERS = 7
NSAMP = 256
NPIX = 256
NCOMP = 3
HITS = 6
TILE_DEV = 32
SPAN_GRP = 16
SPANS = 128
NTILES = 256
ROWS = 24
CAP = 3
N_TM = 8
N_WAFER = 4


def home_table(key):
    return jax.random.permutation(jax.random.fold_in(key, 7), NTILES).astype(jnp.int32)


def draw_tile_home(key, part):
    return home_table(key)


def draw_tile_list(key, part):
    home_slots = home_table(key)
    inverse = jnp.argsort(home_slots).astype(jnp.int32)
    device_count = N_TM * N_WAFER
    slot_count = N_TM * CAP
    key_score = jax.random.fold_in(key, 21)
    key_full = jax.random.fold_in(key, 22)
    key_base = jax.random.fold_in(key, 23)
    key_shuffle = jax.random.fold_in(key, 24)
    positions = jnp.arange(slot_count, dtype=jnp.int32)
    scores = jax.random.randint(key_score, (device_count, slot_count), 0, 1 << 20) * slot_count + positions[None, :]
    full_owner = jax.random.randint(key_full, (N_WAFER,), 0, N_TM)
    device_full = full_owner[jnp.arange(device_count, dtype=jnp.int32) % N_WAFER]
    forced = (positions // CAP)[None, :] == device_full[:, None]
    scores = jnp.where(forced, scores - (1 << 28), scores)
    picked = jnp.argsort(scores, axis=1)[:, :ROWS].astype(jnp.int32)
    row_index = jnp.arange(ROWS, dtype=jnp.int32)
    shuffle_scores = jax.random.randint(key_shuffle, (device_count, ROWS), 0, 1 << 20) * ROWS + row_index[None, :]
    shuffle_order = jnp.argsort(shuffle_scores, axis=1)
    picked = jnp.take_along_axis(picked, shuffle_order, axis=1)
    owner_pick = picked // CAP
    rank_pick = picked % CAP
    base_slot = jax.random.randint(key_base, (device_count, N_TM), 0, TILE_DEV)
    base_pick = jnp.take_along_axis(base_slot, owner_pick, axis=1)
    local_slot = (base_pick + rank_pick) % TILE_DEV
    slot_rows = owner_pick * TILE_DEV + local_slot
    tile_ids = jnp.take(inverse, slot_rows.reshape(-1), axis=0)
    return tile_ids.reshape(SPANS, HITS).astype(jnp.int32)


def draw_whiten(key, part):
    key_off = jax.random.fold_in(key, 3)
    key_diag = jax.random.fold_in(key, 4)
    spread = 0.35
    lower_end = 0.75
    upper_end = 1.25
    uniform_part = jax.random.uniform(key_off, (WAFERS, WDET, WDET), jnp.float32, -1.0, 1.0)
    symmetric = (uniform_part + jnp.swapaxes(uniform_part, 1, 2)) * (spread / math.sqrt(WDET))
    diagonal = jax.random.uniform(key_diag, (WAFERS, WDET), jnp.float32, lower_end, upper_end)
    identity = jnp.eye(WDET, dtype=jnp.float32)
    return (symmetric * (1.0 - identity)[None, :, :] + identity[None, :, :] * diagonal[:, None, :]).astype(jnp.bfloat16)


def draw_sample_weight(key, part):
    run_count = SPANS * NSAMP // 16
    key_level = jax.random.fold_in(key, 41)
    key_jitter = jax.random.fold_in(key, 42)
    key_cut = jax.random.fold_in(key, 43)
    level = jax.random.uniform(key_level, (WDET, 1, 1), jnp.float32, 0.5, 2.0)
    jitter = jax.random.uniform(key_jitter, (WDET, run_count, 16), jnp.float32, 0.6, 1.4)
    kept = (jax.random.randint(key_cut, (WDET, run_count, 1), 0, 8) != 0).astype(jnp.float32)
    return (level * jitter * kept).reshape(WDET, SPANS * NSAMP).astype(jnp.bfloat16)


def with_ends(result, own_key, low, high):
    longest = result.shape.index(max(result.shape))
    spots = []
    for shift in (0, 1):
        where = [jax.random.randint(jax.random.fold_in(own_key, axis), (), 0, length) for axis, length in enumerate(result.shape)]
        where[longest] = (where[longest] + shift) % result.shape[longest]
        spots.append(tuple(where))
    return result.at[spots[0]].set(low).at[spots[1]].set(high)


def shard_levels(stream_key, shape, cuts, least, high):
    loudness, own = 1.0, jax.random.fold_in(stream_key, 6)
    for axis_at, blocks in cuts:
        steps = jnp.exp(jax.random.uniform(jax.random.fold_in(own, axis_at), (blocks,), jnp.float32, least / len(cuts), high / len(cuts)))
        loudness = loudness * jnp.repeat(steps, shape[axis_at] // blocks).reshape([-1 if axis == axis_at else 1 for axis in range(len(shape))])
    return loudness


def gaussian(key, extent, scale, bound, split=(), kind=jnp.bfloat16):
    drawn = jax.random.normal(key, extent, jnp.float32) * scale
    if len(split) > 0:
        drawn = shard_levels(key, extent, split, -0.22, 0.18) * drawn
    return jnp.clip(drawn, min=-bound, max=bound).astype(kind)


def setup_inputs(seed: int = 0) -> dict:
    keys = jax.random.split(jax.random.key(seed), 13)
    timestream = gaussian(keys[0], (WDET, SPANS * NSAMP), 1.0, 6.0, ((0, 4), (1, 8)))
    sample_weight = draw_sample_weight(jax.random.fold_in(keys[12], 71), 0)
    response = jnp.clip(jax.random.uniform(keys[2], (NCOMP, WDET), jnp.float32, -1.0, 1.0), -1.0, 1.0)
    band_filter = gaussian(keys[3], (NSAMP, NSAMP), NSAMP ** -0.5, 0.375)
    whiten = draw_whiten(jax.random.fold_in(keys[12], 71), 0)
    group_wafer = with_ends(jax.random.randint(keys[5], (N_TM,), 0, WAFERS), jax.random.fold_in(keys[5], 1), 0, WAFERS - 1).astype(jnp.int32)
    pointing = gaussian(keys[6], (SPANS, HITS, NSAMP, NPIX), (HITS * NPIX) ** -0.5, 0.15625, ((0, 32),))
    tile_list = draw_tile_list(jax.random.fold_in(keys[12], 71), 0)
    tile_home = draw_tile_home(jax.random.fold_in(keys[12], 71), 0)
    solution = gaussian(keys[9], (NTILES, NCOMP, NPIX), 1.0, 6.0, ((0, 8),), jnp.float32)
    direction = gaussian(keys[10], (NTILES, NCOMP, NPIX), 1.0, 6.0, ((0, 8),), jnp.float32)
    cg_scalars = jnp.clip(jax.random.uniform(keys[11], (2,), jnp.float32, 0.5, 1.5), 0.5, 1.5)
    return {"timestream": timestream, "sample_weight": sample_weight, "response": response, "band_filter": band_filter, "whiten": whiten, "group_wafer": group_wafer, "pointing": pointing, "tile_list": tile_list, "tile_home": tile_home, "solution": solution, "direction": direction, "cg_scalars": cg_scalars}


def reference(timestream, sample_weight, response, band_filter, whiten, group_wafer, pointing, tile_list, tile_home, solution, direction, cg_scalars):
    precise_mode = lax.Precision.HIGHEST
    step_size = cg_scalars[0]
    blend_weight = cg_scalars[1]
    updated = solution + step_size * direction
    short_map = updated.astype(jnp.bfloat16)
    home_rows = jnp.take(tile_home, tile_list, axis=0).astype(jnp.int32)
    group_width = SPAN_GRP * NSAMP

    def group_term(group_idx):
        group_idx = group_idx.astype(jnp.int32)
        first_span = (group_idx * SPAN_GRP).astype(jnp.int32)
        first_sample = (group_idx * group_width).astype(jnp.int32)
        samples_grp = lax.dynamic_slice_in_dim(timestream, first_sample, group_width, 1).astype(jnp.float32)
        samples_grp = samples_grp.reshape(WDET, SPAN_GRP, NSAMP)
        weight_grp = lax.dynamic_slice_in_dim(sample_weight, first_sample, group_width, 1).astype(jnp.float32)
        weight_grp = weight_grp.reshape(WDET, SPAN_GRP, NSAMP)
        weights = lax.dynamic_slice_in_dim(pointing, first_span, SPAN_GRP, 0).astype(jnp.float32)
        rows_here = lax.dynamic_slice_in_dim(home_rows, first_span, SPAN_GRP, 0)
        tile_vals = jnp.take(short_map, rows_here, axis=0).astype(jnp.float32)
        signal_parts = jnp.einsum("cktp,ckjp->cjt", weights, tile_vals, precision=precise_mode)
        signal = jnp.einsum("jd,cjt->dct", response, signal_parts, precision=precise_mode)
        errors = ((samples_grp - signal) * weight_grp).astype(jnp.bfloat16)
        filtered = jnp.dot(errors.reshape(WDET * SPAN_GRP, NSAMP), band_filter, preferred_element_type=jnp.float32)
        filtered = filtered.astype(jnp.bfloat16).reshape(WDET, group_width)
        matrix = lax.dynamic_index_in_dim(whiten, group_wafer[group_idx], 0, keepdims=False)
        whitened = jnp.dot(matrix, filtered, preferred_element_type=jnp.float32).astype(jnp.bfloat16)
        smoothed = jnp.dot(whitened.reshape(WDET * SPAN_GRP, NSAMP), band_filter.T, preferred_element_type=jnp.float32)
        smoothed = smoothed.astype(jnp.bfloat16).reshape(WDET, SPAN_GRP, NSAMP)
        stokes = jnp.einsum("jd,dct->cjt", response, smoothed.astype(jnp.float32) * weight_grp, precision=precise_mode)
        stokes = stokes.astype(jnp.bfloat16)
        return jnp.einsum("cjt,cktp->ckjp", stokes.astype(jnp.float32), weights, precision=precise_mode)

    partials = lax.map(group_term, jnp.arange(N_TM, dtype=jnp.int32))
    summed = jax.ops.segment_sum(partials.reshape(SPANS * HITS, NCOMP, NPIX), home_rows.reshape(SPANS * HITS), num_segments=NTILES)
    residual_next = summed * (float(WDET) ** -0.5)
    direction_next = residual_next + blend_weight * direction
    return (updated, residual_next, direction_next)
```

```python
import functools

import jax
import jax.numpy as jnp
from jax import lax
from jax.experimental import pallas as pl
from jax.experimental.pallas import tpu as pltpu
from jax.sharding import PartitionSpec as P

MESH = pl.DeviceIdType.MESH
F32 = jnp.float32
BF16 = jnp.bfloat16


def body(dims, *refs):
    n_tm, n_wf, det, spans, hits, samples, pixels, tiles_own, pack, gather_w = dims
    (ts, sw, whiten, picks, point_in, band, resp, short, hr8, src, ids) = refs[:11]
    out = refs[11]
    (tsb, swb, wsel, wbuf, point, mapb, idb, fs, sig, filt, part, outb, arrb, sums) = refs[12:26]
    (loc, s_ts, r_ts, s_sw, r_sw, s_w1, r_w1, s_w2, r_w2, s_map, r_map, s_id, r_id, s_out, r_out, s_sum, r_sum) = refs[26:]
    t = lax.axis_index("tm")
    w = lax.axis_index("wafer")
    det_own = det // n_wf
    rows = spans * hits
    part_rows = rows * 8
    all_tiles = n_tm * tiles_own

    def tm_to(d):
        return lax.rem(t + d, n_tm)

    def tm_from(d):
        return lax.rem(t + n_tm - d, n_tm)

    def remote(src_ref, dst_ref, send, recv, device):
        return pltpu.make_async_remote_copy(
            src_ref=src_ref, dst_ref=dst_ref, send_sem=send, recv_sem=recv, device_id=device, device_id_type=MESH
        )

    def over_tm(step):
        def run(i, carry):
            step(i + 1)
            return carry

        lax.fori_loop(0, n_tm - 1, run, 0)

    def own_chunk(s):
        cols = pl.ds(pl.multiple_of((w * spans + s) * samples, samples), samples)
        here = pl.ds(pl.multiple_of(w * det_own, det_own), det_own)
        return (
            pltpu.make_async_copy(ts.at[:, cols], tsb.at[s, here, :], loc.at[s]),
            pltpu.make_async_copy(sw.at[:, cols], swb.at[s, here, :], loc.at[spans + s]),
        )

    own_map = pltpu.make_async_copy(short, mapb.at[t], loc.at[2 * spans])
    own_ids = pltpu.make_async_copy(ids.at[t], idb.at[t], loc.at[2 * spans + 1])
    for s in range(spans):
        for copy in own_chunk(s):
            copy.start()
    own_map.start()
    own_ids.start()
    own_point = pltpu.make_async_copy(point_in, point, loc.at[2 * spans + 4])
    own_point.start()
    if gather_w:
        for g in range(n_tm):
            wsel[g] = whiten[picks[g]]
        own_w = pltpu.make_async_copy(wsel.at[t], wbuf.at[t, w], loc.at[2 * spans + 2])
        own_w.start()

    barrier = pltpu.get_barrier_semaphore()

    def greet(d):
        pl.semaphore_signal(barrier, inc=1, device_id=(tm_to(d), w), device_id_type=MESH)

    over_tm(greet)
    for d in range(1, n_wf):
        pl.semaphore_signal(barrier, inc=1, device_id=(t, lax.rem(w + d, n_wf)), device_id_type=MESH)
    pl.semaphore_wait(barrier, n_tm - 1 + n_wf - 1)

    def map_out(d):
        return remote(short, mapb.at[t], s_map.at[d], r_map.at[d], (tm_to(d), w))

    def map_in(d):
        return remote(short, mapb.at[tm_from(d)], s_map.at[d], r_map.at[d], (tm_to(d), w))

    def id_out(d):
        return remote(ids.at[tm_to(d)], idb.at[t], s_id.at[d], r_id.at[d], (tm_to(d), w))

    def id_in(d):
        return remote(ids.at[tm_to(d)], idb.at[tm_from(d)], s_id.at[d], r_id.at[d], (tm_to(d), w))

    def w1_out(d):
        return remote(wsel.at[tm_to(d)], wbuf.at[t, w], s_w1.at[d], r_w1.at[d], (tm_to(d), w))

    def w1_in(d):
        return remote(wsel.at[tm_to(d)], wbuf.at[tm_from(d), w], s_w1.at[d], r_w1.at[d], (tm_to(d), w))

    def chunk(s, d, arriving):
        to = lax.rem(w + d, n_wf)
        row = lax.rem(w + n_wf - d, n_wf) if arriving else w
        cols = pl.ds(pl.multiple_of((to * spans + s) * samples, samples), samples)
        there = pl.ds(pl.multiple_of(row * det_own, det_own), det_own)
        return (
            remote(ts.at[:, cols], tsb.at[s, there, :], s_ts.at[s, d], r_ts.at[s, d], (t, to)),
            remote(sw.at[:, cols], swb.at[s, there, :], s_sw.at[s, d], r_sw.at[s, d], (t, to)),
        )

    def send_span(s):
        for d in range(1, n_wf):
            for copy in chunk(s, d, False):
                copy.start()

    over_tm(lambda d: map_out(d).start())
    if gather_w:
        over_tm(lambda d: w1_out(d).start())
    over_tm(lambda d: id_out(d).start())
    early = spans // 2 if gather_w else spans
    for s in range(early):
        send_span(s)

    own_map.wait()
    over_tm(lambda d: map_in(d).wait_recv())
    at = lax.broadcasted_iota(jnp.int32, (part_rows, all_tiles), 1)
    comp = lax.rem(lax.broadcasted_iota(jnp.int32, (part_rows, all_tiles), 0), 8)
    named = at == hr8[...]
    total = jnp.zeros((part_rows, pixels), F32)
    for j in range(3):
        pick = jnp.where(named & (comp == j), 1.0, 0.0).astype(BF16)
        plane = mapb[:, j].reshape(all_tiles, pixels)
        total += jnp.dot(pick, plane, preferred_element_type=F32)
    fs[...] = total
    own_point.wait()

    if gather_w:
        own_w.wait()
        over_tm(lambda d: w1_in(d).wait_recv())
        mate = w + 1 - 2 * lax.rem(w, 2)
        far = lax.rem(w + 2, n_wf)
        far_mate = far + 1 - 2 * lax.rem(far, 2)

        def w2(kind, arriving):
            who = (mate, far, mate)[kind]
            block = ((mate, far, far_mate) if arriving else (w, w, far))[kind]
            return remote(wbuf.at[:, block], wbuf.at[:, block], s_w2.at[kind], r_w2.at[kind], (t, who))

        w2(1, False).start()
        w2(0, False).start()
        for s in range(early, spans):
            send_span(s)

    def signal_of(c, carry):
        acc = jnp.zeros((8, samples), F32)
        for k in range(hits):
            tile = fs[pl.ds(pl.multiple_of((c * hits + k) * 8, 8), 8), :].astype(BF16)
            acc += lax.dot_general(tile, point[c, k], (((1,), (1,)), ((), ())), preferred_element_type=F32)
        sig[c] = acc
        return carry

    lax.fori_loop(0, spans, signal_of, 0)

    if gather_w:
        w2(1, True).wait_recv()
        w2(2, False).start()
        w2(0, True).wait_recv()
        w2(2, True).wait_recv()

    block = 256
    per_block = block * n_tm // det

    def weights_at(i):
        if gather_w:
            return wbuf[pl.ds(i * per_block, per_block)].reshape(block, det)
        return whiten[pl.ds(pl.multiple_of(i * block, block), block), :]

    def one_span(s, carry):
        for copy in own_chunk(s):
            copy.wait()
        for d in range(1, n_wf):
            for copy in chunk(s, d, True):
                copy.wait_recv()
        srow = sig[s]

        def first(i, carry):
            here = pl.ds(pl.multiple_of(i * block, block), block)
            r = resp[here, :]
            signal = r[:, 0:1] * srow[0:1] + r[:, 1:2] * srow[1:2] + r[:, 2:3] * srow[2:3]
            err = (tsb[s, here, :].astype(F32) - signal) * swb[s, here, :].astype(F32)
            filt[here, :] = jnp.dot(err.astype(BF16), band[...], preferred_element_type=F32).astype(BF16)
            return carry

        lax.fori_loop(0, det // block, first, 0)

        def second(i, acc):
            here = pl.ds(pl.multiple_of(i * block, block), block)
            white = jnp.dot(weights_at(i), filt[...], preferred_element_type=F32).astype(BF16)
            smooth = lax.dot_general(white, band[...], (((1,), (1,)), ((), ())), preferred_element_type=F32)
            x = smooth.astype(BF16).astype(F32) * swb[s, here, :].astype(F32)
            r = resp[here, :]
            return tuple(a + jnp.sum(x * r[:, j : j + 1], axis=0, keepdims=True) for j, a in enumerate(acc))

        zero = jnp.zeros((1, samples), F32)
        acc = lax.fori_loop(0, det // block, second, (zero, zero, zero))
        stokes = jnp.concatenate([*acc, jnp.zeros((5, samples), F32)], axis=0).astype(BF16)
        for k in range(hits):
            there = pl.ds(pl.multiple_of((s * hits + k) * 8, 8), 8)
            part[there, :] = jnp.dot(stokes, point[s, k], preferred_element_type=F32)
        return carry

    lax.fori_loop(0, spans, one_span, 0)

    col = lax.broadcasted_iota(jnp.int32, (n_tm * pack, part_rows), 1)
    place = jnp.where(col == src[...], 1.0, 0.0)
    outb[...] = jnp.dot(place, part[...], preferred_element_type=F32, precision=lax.Precision.HIGHEST).reshape(
        n_tm, pack, pixels
    )
    own_out = pltpu.make_async_copy(outb.at[t], arrb.at[t], loc.at[2 * spans + 3])
    own_out.start()

    def sum_out(d):
        return remote(outb.at[tm_to(d)], arrb.at[t], s_out.at[d], r_out.at[d], (tm_to(d), w))

    def sum_in(d):
        return remote(outb.at[tm_to(d)], arrb.at[tm_from(d)], s_out.at[d], r_out.at[d], (tm_to(d), w))

    over_tm(lambda d: sum_out(d).start())
    own_ids.wait()
    over_tm(lambda d: id_in(d).wait_recv())
    width = 3 * tiles_own
    lanes = idb.shape[2]
    spot = lax.broadcasted_iota(jnp.int32, (n_tm * pack, lanes), 1).astype(F32)
    hit = jnp.where(idb[...].reshape(n_tm * pack, lanes) == spot, 1.0, 0.0)
    own_out.wait()
    over_tm(lambda d: sum_in(d).wait_recv())
    owned = lax.dot_general(
        hit,
        arrb[...].reshape(n_tm * pack, pixels),
        (((0,), (0,)), ((), ())),
        preferred_element_type=F32,
        precision=lax.Precision.HIGHEST,
    )
    sums[w] = owned[:width]

    def share(d, arriving):
        to = lax.rem(w + d, n_wf)
        slot = lax.rem(w + n_wf - d, n_wf) if arriving else w
        return remote(sums.at[w], sums.at[slot], s_sum.at[d], r_sum.at[d], (t, to))

    for d in range(1, n_wf):
        share(d, False).start()
    for d in range(1, n_wf):
        share(d, True).wait_recv()
    result = sums[0]
    for i in range(1, n_wf):
        result = result + sums[i]
    out[...] = result

    def sent(d):
        map_out(d).wait_send()
        id_out(d).wait_send()
        if gather_w:
            w1_out(d).wait_send()
        sum_out(d).wait_send()

    over_tm(sent)
    for d in range(1, n_wf):
        share(d, False).wait_send()

    def spans_sent(s, carry):
        for d in range(1, n_wf):
            for copy in chunk(s, d, False):
                copy.wait_send()
        return carry

    lax.fori_loop(0, spans, spans_sent, 0)
    if gather_w:
        for kind in range(3):
            w2(kind, False).wait_send()


def shards(
    timestream,
    sample_weight,
    response,
    band_filter,
    whiten,
    group_wafer,
    pointing,
    tile_list,
    tile_home,
    solution,
    direction,
    cg_scalars,
):
    n_tm = lax.axis_size("tm")
    n_wf = lax.axis_size("wafer")
    updated = solution + cg_scalars[0] * direction
    tiles_own, comps, pixels = solution.shape
    spans, hits = tile_list.shape
    samples = band_filter.shape[0]
    w_rows, det = whiten.shape[1:]
    rows = spans * hits
    cap = max(2, (rows + n_tm - 1) // n_tm)
    pack = (3 * cap + 7) // 8 * 8
    all_tiles = tile_home.shape[0]
    short = updated.astype(BF16).transpose(1, 0, 2)

    ids_here = tile_list.reshape(rows)
    home = jnp.sum(
        jnp.where(ids_here[:, None] == jnp.arange(all_tiles, dtype=jnp.int32)[None, :], tile_home[None, :], 0), axis=1
    )
    owner = home // tiles_own
    local = home % tiles_own
    order = jnp.arange(rows, dtype=jnp.int32)
    before = jnp.sum(((owner[:, None] == owner[None, :]) & (order[None, :] < order[:, None])).astype(jnp.int32), axis=1)
    m = jnp.arange(n_tm * pack, dtype=jnp.int32)
    slot, comp = (m % pack) // 3, (m % pack) % 3
    match = (
        (owner[None, :] == (m // pack)[:, None]) & (before[None, :] == slot[:, None]) & (slot < cap)[:, None]
    )
    src = jnp.sum(jnp.where(match, order[None, :] * 8 + comp[:, None] + 1, 0), axis=1) - 1
    ids = jnp.sum(jnp.where(match, local[None, :] + comp[:, None] * tiles_own + 1, 0), axis=1) - 1
    lanes = (3 * tiles_own + 127) // 128 * 128
    ids = jnp.broadcast_to(ids.astype(F32).reshape(n_tm, pack, 1), (n_tm, pack, lanes))
    hr8 = jnp.broadcast_to(home[:, None], (rows, 8)).reshape(rows * 8, 1)

    gather_w = w_rows % 16 == 0 and n_wf == 4 and 256 * n_tm % det == 0
    if not gather_w:
        wsel = sum(jnp.where((group_wafer == v)[:, None, None], whiten[v][None], 0) for v in range(whiten.shape[0]))
        mine = lax.all_to_all(wsel, "tm", split_axis=0, concat_axis=0, tiled=True)
        whiten = lax.all_gather(mine, "wafer", axis=1, tiled=True).reshape(det, det)

    any_space = pl.BlockSpec(memory_space=pl.ANY)
    vmem = pl.BlockSpec(memory_space=pltpu.VMEM)
    dma = pltpu.SemaphoreType.DMA
    dims = (n_tm, n_wf, det, spans, hits, samples, pixels, tiles_own, pack, gather_w)
    part_rows = rows * 8
    w_shape = (n_tm, n_wf, w_rows, det) if gather_w else (1, 1, 16, 128)
    summed = pl.pallas_call(
        functools.partial(body, dims),
        out_shape=jax.ShapeDtypeStruct((3 * tiles_own, pixels), F32),
        in_specs=[any_space, any_space, vmem, pl.BlockSpec(memory_space=pltpu.SMEM), any_space] + [vmem] * 6,
        out_specs=vmem,
        scratch_shapes=[
            pltpu.VMEM((spans, det, samples), BF16),
            pltpu.VMEM((spans, det, samples), BF16),
            pltpu.VMEM((n_tm, w_rows, det) if gather_w else (1, 16, 128), BF16),
            pltpu.VMEM(w_shape, BF16),
            pltpu.VMEM(pointing.shape, BF16),
            pltpu.VMEM((n_tm, 3, tiles_own, pixels), BF16),
            pltpu.VMEM((n_tm, pack, lanes), F32),
            pltpu.VMEM((part_rows, pixels), F32),
            pltpu.VMEM((spans, 8, samples), F32),
            pltpu.VMEM((det, samples), BF16),
            pltpu.VMEM((part_rows, pixels), F32),
            pltpu.VMEM((n_tm, pack, pixels), F32),
            pltpu.VMEM((n_tm, pack, pixels), F32),
            pltpu.VMEM((n_wf, 3 * tiles_own, pixels), F32),
            dma((2 * spans + 5,)),
            dma((spans, n_wf)),
            dma((spans, n_wf)),
            dma((spans, n_wf)),
            dma((spans, n_wf)),
            dma((n_tm,)),
            dma((n_tm,)),
            dma((3,)),
            dma((3,)),
            dma((n_tm,)),
            dma((n_tm,)),
            dma((n_tm,)),
            dma((n_tm,)),
            dma((n_tm,)),
            dma((n_tm,)),
            dma((n_wf,)),
            dma((n_wf,)),
        ],
        compiler_params=pltpu.CompilerParams(
            collective_id=0, has_side_effects=True, vmem_limit_bytes=56 * 1024 * 1024
        ),
    )(
        timestream,
        sample_weight,
        whiten,
        group_wafer,
        pointing,
        band_filter,
        response.T,
        short,
        hr8,
        src[:, None],
        ids,
    )
    summed = summed.reshape(3, tiles_own, pixels).transpose(1, 0, 2)
    residual_next = summed * float(det) ** (-0.5)
    direction_next = residual_next + cg_scalars[1] * direction
    return (updated, residual_next, direction_next)


def solution(mesh):
    in_specs = (
        P("wafer", "tm"),
        P("wafer", "tm"),
        P(),
        P(),
        P(None, ("tm", "wafer"), None),
        P(),
        P(("tm", "wafer"), None, None, None),
        P(("tm", "wafer"), None),
        P(),
        P("tm", None, None),
        P("tm", None, None),
        P(),
    )
    out_specs = (P("tm", None, None), P("tm", None, None), P("tm", None, None))
    return jax.shard_map(shards, mesh=mesh, in_specs=in_specs, out_specs=out_specs, check_vma=False)
```

```python
import functools

import jax
import jax.numpy as jnp
from jax import lax
from jax.experimental import pallas as pl
from jax.experimental.pallas import tpu as pltpu
from jax.sharding import PartitionSpec as P

MESH = pl.DeviceIdType.MESH
F32 = jnp.float32
BF16 = jnp.bfloat16
EARLY = 2
CHAIN = True


def body(dims, *refs):
    n_tm, n_wf, det, spans, hits, samples, pixels, tiles_own, pack, gather_w = dims
    (ts, sw, whiten, picks, point_in, band, resp_in, sky, way, scal, tiles, homes) = refs[:12]
    (out_sky, out_res, out_way) = refs[12:15]
    (tsb, swb, wsel, wbuf, point, mapb, idb, fs, sig, filt, part, outb, arrb, sums, short, ids, resp) = refs[15:32]
    (loc, s_ts, r_ts, s_sw, r_sw, s_w1, r_w1, s_w2, r_w2, s_map, r_map, s_id, r_id, s_out, r_out, s_sum, r_sum) = refs[32:]
    t = lax.axis_index("tm")
    w = lax.axis_index("wafer")
    det_own = det // n_wf
    rows = spans * hits
    part_rows = rows * 8
    all_tiles = n_tm * tiles_own

    def tm_to(d):
        return lax.rem(t + d, n_tm)

    def tm_from(d):
        return lax.rem(t + n_tm - d, n_tm)

    def remote(src_ref, dst_ref, send, recv, device):
        return pltpu.make_async_remote_copy(
            src_ref=src_ref, dst_ref=dst_ref, send_sem=send, recv_sem=recv, device_id=device, device_id_type=MESH
        )

    def over_tm(step):
        def run(i, carry):
            step(i + 1)
            return carry

        lax.fori_loop(0, n_tm - 1, run, 0)

    def own_chunk(s):
        cols = pl.ds(pl.multiple_of((w * spans + s) * samples, samples), samples)
        here = pl.ds(pl.multiple_of(w * det_own, det_own), det_own)
        return (
            pltpu.make_async_copy(ts.at[:, cols], tsb.at[s, here, :], loc.at[s]),
            pltpu.make_async_copy(sw.at[:, cols], swb.at[s, here, :], loc.at[spans + s]),
        )

    own_map = pltpu.make_async_copy(short, mapb.at[t], loc.at[2 * spans])
    own_ids = pltpu.make_async_copy(ids.at[t], idb.at[t], loc.at[2 * spans + 1])
    for s in range(spans):
        for copy in own_chunk(s):
            copy.start()
    fresh = sky[...] + scal[0] * way[...]
    out_sky[...] = fresh
    short[...] = fresh.astype(BF16)
    own_map.start()
    own_point = pltpu.make_async_copy(point_in, point, loc.at[2 * spans + 4])
    own_point.start()
    if gather_w:
        for g in range(n_tm):
            wsel[g] = whiten[picks[g]]
        own_w = pltpu.make_async_copy(wsel.at[t], wbuf.at[t, w], loc.at[2 * spans + 2])
        own_w.start()

    barrier = pltpu.get_barrier_semaphore()

    def greet(d):
        pl.semaphore_signal(barrier, inc=1, device_id=(tm_to(d), w), device_id_type=MESH)

    over_tm(greet)
    for d in range(1, n_wf):
        pl.semaphore_signal(barrier, inc=1, device_id=(t, lax.rem(w + d, n_wf)), device_id_type=MESH)
    pl.semaphore_wait(barrier, n_tm - 1 + n_wf - 1)

    def map_out(d):
        return remote(short, mapb.at[t], s_map.at[d], r_map.at[d], (tm_to(d), w))

    def map_in(d):
        return remote(short, mapb.at[tm_from(d)], s_map.at[d], r_map.at[d], (tm_to(d), w))

    def id_out(d):
        return remote(ids.at[tm_to(d)], idb.at[t], s_id.at[d], r_id.at[d], (tm_to(d), w))

    def id_in(d):
        return remote(ids.at[tm_to(d)], idb.at[tm_from(d)], s_id.at[d], r_id.at[d], (tm_to(d), w))

    def w1_out(d):
        return remote(wsel.at[tm_to(d)], wbuf.at[t, w], s_w1.at[d], r_w1.at[d], (tm_to(d), w))

    def w1_in(d):
        return remote(wsel.at[tm_to(d)], wbuf.at[tm_from(d), w], s_w1.at[d], r_w1.at[d], (tm_to(d), w))

    def chunk(s, d, arriving):
        to = lax.rem(w + d, n_wf)
        row = lax.rem(w + n_wf - d, n_wf) if arriving else w
        cols = pl.ds(pl.multiple_of((to * spans + s) * samples, samples), samples)
        there = pl.ds(pl.multiple_of(row * det_own, det_own), det_own)
        return (
            remote(ts.at[:, cols], tsb.at[s, there, :], s_ts.at[s, d], r_ts.at[s, d], (t, to)),
            remote(sw.at[:, cols], swb.at[s, there, :], s_sw.at[s, d], r_sw.at[s, d], (t, to)),
        )

    def send_span(s):
        for d in range(1, n_wf):
            for copy in chunk(s, d, False):
                copy.start()

    over_tm(lambda d: map_out(d).start())
    if gather_w:
        over_tm(lambda d: w1_out(d).start())
    early = EARLY if gather_w else spans
    for s in range(early):
        send_span(s)

    resp[...] = jnp.concatenate([resp_in[...], jnp.zeros((5, det), F32)], axis=0).T

    home = [homes[tiles[c, k]] for c in range(spans) for k in range(hits)]
    lane = lax.broadcasted_iota(jnp.int32, (8, part_rows), 1)
    lane_home = jnp.zeros((8, part_rows), jnp.int32)
    for p in range(rows):
        lane_home = jnp.where(lane // 8 == p, home[p], lane_home)
    lane_comp = lane - lane // 8 * 8
    lane_owner = lane_home // tiles_own
    before = jnp.zeros((8, part_rows), jnp.int32)
    for p in range(rows):
        before += jnp.where((lane_owner == home[p] // tiles_own) & (lane // 8 > p), 1, 0)
    lane_row = jnp.where(lane_comp < 3, before * 3 + lane_comp, -1)
    lane_id = (lane_home - lane_owner * tiles_own + lane_comp * tiles_own + 1).astype(F32)
    row8 = lax.broadcasted_iota(jnp.int32, (8, part_rows), 0)
    lanes = idb.shape[2]
    places = []
    for o in range(n_tm):
        for m in range(0, pack, 8):
            place = jnp.where((lane_owner == o) & (lane_row == row8 + m), 1.0, 0.0)
            places.append(place)
            label = jnp.sum(place * lane_id, axis=1, keepdims=True) - 1.0
            ids[o, m : m + 8] = jnp.broadcast_to(label, (8, lanes))
    place = jnp.concatenate(places, axis=0)
    own_ids.start()
    over_tm(lambda d: id_out(d).start())

    at = lax.broadcasted_iota(jnp.int32, (8, all_tiles), 1)
    comp = lax.broadcasted_iota(jnp.int32, (8, all_tiles), 0)
    named = [at == home[p] for p in range(rows)]
    own_map.wait()
    over_tm(lambda d: map_in(d).wait_recv())
    total = jnp.zeros((part_rows, pixels), F32)
    for j in range(3):
        pick = jnp.concatenate([jnp.where(n & (comp == j), 1.0, 0.0) for n in named], axis=0).astype(BF16)
        plane = mapb[:, j * tiles_own : (j + 1) * tiles_own].reshape(all_tiles, pixels)
        total += jnp.dot(pick, plane, preferred_element_type=F32)
    fs[...] = total
    own_point.wait()

    if gather_w:
        own_w.wait()
        over_tm(lambda d: w1_in(d).wait_recv())
        mate = w + 1 - 2 * lax.rem(w, 2)
        far = lax.rem(w + 2, n_wf)
        far_mate = far + 1 - 2 * lax.rem(far, 2)

        def w2(kind, arriving):
            who = (mate, far, mate)[kind]
            block = ((mate, far, far_mate) if arriving else (w, w, far))[kind]
            return remote(wbuf.at[:, block], wbuf.at[:, block], s_w2.at[kind], r_w2.at[kind], (t, who))

        w2(1, False).start()
        w2(0, False).start()
        if not CHAIN:
            for s in range(early, spans):
                send_span(s)

    def signal_of(c, carry):
        acc = jnp.zeros((8, samples), F32)
        for k in range(hits):
            tile = fs[pl.ds(pl.multiple_of((c * hits + k) * 8, 8), 8), :].astype(BF16)
            acc += lax.dot_general(tile, point[c, k], (((1,), (1,)), ((), ())), preferred_element_type=F32)
        sig[c] = acc
        return carry

    lax.fori_loop(0, spans, signal_of, 0)

    if gather_w:
        w2(1, True).wait_recv()
        w2(2, False).start()
        w2(0, True).wait_recv()
        w2(2, True).wait_recv()

    block = 256
    per_block = block * n_tm // det

    def weights_at(i):
        if gather_w:
            return wbuf[pl.ds(i * per_block, per_block)].reshape(block, det)
        return whiten[pl.ds(pl.multiple_of(i * block, block), block), :]

    def one_span(s, carry):
        for copy in own_chunk(s):
            copy.wait()
        for d in range(1, n_wf):
            for copy in chunk(s, d, True):
                copy.wait_recv()
        if gather_w and CHAIN:

            @pl.when(s + early < spans)
            def _():
                send_span(s + early)

        srow = sig[s]

        def first(i, carry):
            here = pl.ds(pl.multiple_of(i * block, block), block)
            r = resp[here, :]
            signal = r[:, 0:1] * srow[0:1] + r[:, 1:2] * srow[1:2] + r[:, 2:3] * srow[2:3]
            err = (tsb[s, here, :].astype(F32) - signal) * swb[s, here, :].astype(F32)
            filt[here, :] = jnp.dot(err.astype(BF16), band[...], preferred_element_type=F32).astype(BF16)
            return carry

        lax.fori_loop(0, det // block, first, 0)

        def second(i, acc):
            here = pl.ds(pl.multiple_of(i * block, block), block)
            white = jnp.dot(weights_at(i), filt[...], preferred_element_type=F32).astype(BF16)
            smooth = lax.dot_general(white, band[...], (((1,), (1,)), ((), ())), preferred_element_type=F32)
            x = smooth.astype(BF16).astype(F32) * swb[s, here, :].astype(F32)
            r = resp[here, :]
            return tuple(a + jnp.sum(x * r[:, j : j + 1], axis=0, keepdims=True) for j, a in enumerate(acc))

        zero = jnp.zeros((1, samples), F32)
        acc = lax.fori_loop(0, det // block, second, (zero, zero, zero))
        stokes = jnp.concatenate([*acc, jnp.zeros((5, samples), F32)], axis=0).astype(BF16)
        for k in range(hits):
            there = pl.ds(pl.multiple_of((s * hits + k) * 8, 8), 8)
            part[there, :] = jnp.dot(stokes, point[s, k], preferred_element_type=F32)
        return carry

    lax.fori_loop(0, spans, one_span, 0)

    outb[...] = jnp.dot(place, part[...], preferred_element_type=F32, precision=lax.Precision.HIGHEST).reshape(
        n_tm, pack, pixels
    )
    own_out = pltpu.make_async_copy(outb.at[t], arrb.at[t], loc.at[2 * spans + 3])
    own_out.start()

    def sum_out(d):
        return remote(outb.at[tm_to(d)], arrb.at[t], s_out.at[d], r_out.at[d], (tm_to(d), w))

    def sum_in(d):
        return remote(outb.at[tm_to(d)], arrb.at[tm_from(d)], s_out.at[d], r_out.at[d], (tm_to(d), w))

    over_tm(lambda d: sum_out(d).start())
    own_ids.wait()
    over_tm(lambda d: id_in(d).wait_recv())
    width = 3 * tiles_own
    spot = lax.broadcasted_iota(jnp.int32, (n_tm * pack, lanes), 1).astype(F32)
    hit = jnp.where(idb[...].reshape(n_tm * pack, lanes) == spot, 1.0, 0.0)
    own_out.wait()
    over_tm(lambda d: sum_in(d).wait_recv())
    owned = lax.dot_general(
        hit,
        arrb[...].reshape(n_tm * pack, pixels),
        (((0,), (0,)), ((), ())),
        preferred_element_type=F32,
        precision=lax.Precision.HIGHEST,
    )
    sums[w] = owned[:width]

    def share(d, arriving):
        to = lax.rem(w + d, n_wf)
        slot = lax.rem(w + n_wf - d, n_wf) if arriving else w
        return remote(sums.at[w], sums.at[slot], s_sum.at[d], r_sum.at[d], (t, to))

    for d in range(1, n_wf):
        share(d, False).start()
    for d in range(1, n_wf):
        share(d, True).wait_recv()
    result = sums[0]
    for i in range(1, n_wf):
        result = result + sums[i]
    result = result * float(det) ** (-0.5)
    out_res[...] = result
    out_way[...] = result + scal[1] * way[...]

    def sent(d):
        map_out(d).wait_send()
        id_out(d).wait_send()
        if gather_w:
            w1_out(d).wait_send()
        sum_out(d).wait_send()

    over_tm(sent)
    for d in range(1, n_wf):
        share(d, False).wait_send()

    def spans_sent(s, carry):
        for d in range(1, n_wf):
            for copy in chunk(s, d, False):
                copy.wait_send()
        return carry

    lax.fori_loop(0, spans, spans_sent, 0)
    if gather_w:
        for kind in range(3):
            w2(kind, False).wait_send()


def shards(
    timestream,
    sample_weight,
    response,
    band_filter,
    whiten,
    group_wafer,
    pointing,
    tile_list,
    tile_home,
    solution,
    direction,
    cg_scalars,
):
    n_tm = lax.axis_size("tm")
    n_wf = lax.axis_size("wafer")
    tiles_own, comps, pixels = solution.shape
    spans, hits = tile_list.shape
    samples = band_filter.shape[0]
    w_rows, det = whiten.shape[1:]
    rows = spans * hits
    cap = max(2, (rows + n_tm - 1) // n_tm)
    pack = (3 * cap + 7) // 8 * 8
    lanes = (3 * tiles_own + 127) // 128 * 128
    gather_w = w_rows % 16 == 0 and n_wf == 4 and 256 * n_tm % det == 0
    if not gather_w:
        wsel = sum(jnp.where((group_wafer == v)[:, None, None], whiten[v][None], 0) for v in range(whiten.shape[0]))
        mine = lax.all_to_all(wsel, "tm", split_axis=0, concat_axis=0, tiled=True)
        whiten = lax.all_gather(mine, "wafer", axis=1, tiled=True).reshape(det, det)

    any_space = pl.BlockSpec(memory_space=pl.ANY)
    vmem = pl.BlockSpec(memory_space=pltpu.VMEM)
    dma = pltpu.SemaphoreType.DMA
    dims = (n_tm, n_wf, det, spans, hits, samples, pixels, tiles_own, pack, gather_w)
    part_rows = rows * 8
    w_shape = (n_tm, n_wf, w_rows, det) if gather_w else (1, 1, 16, 128)
    smem = pl.BlockSpec(memory_space=pltpu.SMEM)
    plane = jax.ShapeDtypeStruct((3 * tiles_own, pixels), F32)
    results = pl.pallas_call(
        functools.partial(body, dims),
        out_shape=[plane] * 3,
        in_specs=[any_space, any_space, vmem, smem, any_space, vmem, vmem, vmem, vmem, smem, smem, smem],
        out_specs=[vmem] * 3,
        scratch_shapes=[
            pltpu.VMEM((spans, det, samples), BF16),
            pltpu.VMEM((spans, det, samples), BF16),
            pltpu.VMEM((n_tm, w_rows, det) if gather_w else (1, 16, 128), BF16),
            pltpu.VMEM(w_shape, BF16),
            pltpu.VMEM(pointing.shape, BF16),
            pltpu.VMEM((n_tm, 3 * tiles_own, pixels), BF16),
            pltpu.VMEM((n_tm, pack, lanes), F32),
            pltpu.VMEM((part_rows, pixels), F32),
            pltpu.VMEM((spans, 8, samples), F32),
            pltpu.VMEM((det, samples), BF16),
            pltpu.VMEM((part_rows, pixels), F32),
            pltpu.VMEM((n_tm, pack, pixels), F32),
            pltpu.VMEM((n_tm, pack, pixels), F32),
            pltpu.VMEM((n_wf, 3 * tiles_own, pixels), F32),
            pltpu.VMEM((3 * tiles_own, pixels), BF16),
            pltpu.VMEM((n_tm, pack, lanes), F32),
            pltpu.VMEM((det, 8), F32),
            dma((2 * spans + 5,)),
            dma((spans, n_wf)),
            dma((spans, n_wf)),
            dma((spans, n_wf)),
            dma((spans, n_wf)),
            dma((n_tm,)),
            dma((n_tm,)),
            dma((3,)),
            dma((3,)),
            dma((n_tm,)),
            dma((n_tm,)),
            dma((n_tm,)),
            dma((n_tm,)),
            dma((n_tm,)),
            dma((n_tm,)),
            dma((n_wf,)),
            dma((n_wf,)),
        ],
        compiler_params=pltpu.CompilerParams(
            collective_id=0, has_side_effects=True, vmem_limit_bytes=56 * 1024 * 1024
        ),
    )(
        timestream,
        sample_weight,
        whiten,
        group_wafer,
        pointing,
        band_filter,
        response,
        solution.transpose(1, 0, 2).reshape(3 * tiles_own, pixels),
        direction.transpose(1, 0, 2).reshape(3 * tiles_own, pixels),
        cg_scalars,
        tile_list,
        tile_home,
    )
    return tuple(x.reshape(3, tiles_own, pixels).transpose(1, 0, 2) for x in results)


def solution(mesh):
    in_specs = (
        P("wafer", "tm"),
        P("wafer", "tm"),
        P(),
        P(),
        P(None, ("tm", "wafer"), None),
        P(),
        P(("tm", "wafer"), None, None, None),
        P(("tm", "wafer"), None),
        P(),
        P("tm", None, None),
        P("tm", None, None),
        P(),
    )
    out_specs = (P("tm", None, None), P("tm", None, None), P("tm", None, None))
    return jax.shard_map(shards, mesh=mesh, in_specs=in_specs, out_specs=out_specs, check_vma=False)
```

```python
import functools

import jax
import jax.numpy as jnp
from jax import lax
from jax.experimental import pallas as pl
from jax.experimental.pallas import tpu as pltpu
from jax.sharding import PartitionSpec as P

MESH = pl.DeviceIdType.MESH
F32 = jnp.float32
BF16 = jnp.bfloat16
EARLY = 2
CHAIN = False


def body(dims, *refs):
    n_tm, n_wf, det, spans, hits, samples, pixels, tiles_own, pack, gather_w = dims
    (ts, sw, whiten, picks, point_in, band, resp_in, sky, way, scal, tiles, homes) = refs[:12]
    (out_sky, out_res, out_way) = refs[12:15]
    (tsb, swb, wsel, wbuf, point, mapb, idb, fs, sig, filt, part, outb, arrb, sums, short, ids, resp) = refs[15:32]
    (loc, s_ts, r_ts, s_sw, r_sw, s_w1, r_w1, s_w2, r_w2, s_map, r_map, s_id, r_id, s_out, r_out, s_sum, r_sum) = refs[32:]
    t = lax.axis_index("tm")
    w = lax.axis_index("wafer")
    det_own = det // n_wf
    rows = spans * hits
    part_rows = rows * 8
    all_tiles = n_tm * tiles_own

    def tm_to(d):
        return lax.rem(t + d, n_tm)

    def tm_from(d):
        return lax.rem(t + n_tm - d, n_tm)

    def remote(src_ref, dst_ref, send, recv, device):
        return pltpu.make_async_remote_copy(
            src_ref=src_ref, dst_ref=dst_ref, send_sem=send, recv_sem=recv, device_id=device, device_id_type=MESH
        )

    def over_tm(step):
        def run(i, carry):
            step(i + 1)
            return carry

        lax.fori_loop(0, n_tm - 1, run, 0)

    def own_chunk(s):
        cols = pl.ds(pl.multiple_of((w * spans + s) * samples, samples), samples)
        here = pl.ds(pl.multiple_of(w * det_own, det_own), det_own)
        return (
            pltpu.make_async_copy(ts.at[:, cols], tsb.at[s, here, :], loc.at[s]),
            pltpu.make_async_copy(sw.at[:, cols], swb.at[s, here, :], loc.at[spans + s]),
        )

    own_map = pltpu.make_async_copy(short, mapb.at[t], loc.at[2 * spans])
    own_ids = pltpu.make_async_copy(ids.at[t], idb.at[t], loc.at[2 * spans + 1])
    for s in range(spans):
        for copy in own_chunk(s):
            copy.start()
    fresh = sky[...] + scal[0] * way[...]
    out_sky[...] = fresh
    short[...] = fresh.astype(BF16)
    own_map.start()
    own_point = pltpu.make_async_copy(point_in, point, loc.at[2 * spans + 4])
    own_point.start()
    if gather_w:
        for g in range(n_tm):
            wsel[g] = whiten[picks[g]]
        own_w = pltpu.make_async_copy(wsel.at[t], wbuf.at[t, w], loc.at[2 * spans + 2])
        own_w.start()

    barrier = pltpu.get_barrier_semaphore()

    def greet(d):
        pl.semaphore_signal(barrier, inc=1, device_id=(tm_to(d), w), device_id_type=MESH)

    over_tm(greet)
    for d in range(1, n_wf):
        pl.semaphore_signal(barrier, inc=1, device_id=(t, lax.rem(w + d, n_wf)), device_id_type=MESH)
    pl.semaphore_wait(barrier, n_tm - 1 + n_wf - 1)

    def map_out(d):
        return remote(short, mapb.at[t], s_map.at[d], r_map.at[d], (tm_to(d), w))

    def map_in(d):
        return remote(short, mapb.at[tm_from(d)], s_map.at[d], r_map.at[d], (tm_to(d), w))

    def id_out(d):
        return remote(ids.at[tm_to(d)], idb.at[t], s_id.at[d], r_id.at[d], (tm_to(d), w))

    def id_in(d):
        return remote(ids.at[tm_to(d)], idb.at[tm_from(d)], s_id.at[d], r_id.at[d], (tm_to(d), w))

    def w1_out(d):
        return remote(wsel.at[tm_to(d)], wbuf.at[t, w], s_w1.at[d], r_w1.at[d], (tm_to(d), w))

    def w1_in(d):
        return remote(wsel.at[tm_to(d)], wbuf.at[tm_from(d), w], s_w1.at[d], r_w1.at[d], (tm_to(d), w))

    def chunk(s, d, arriving):
        to = lax.rem(w + d, n_wf)
        row = lax.rem(w + n_wf - d, n_wf) if arriving else w
        cols = pl.ds(pl.multiple_of((to * spans + s) * samples, samples), samples)
        there = pl.ds(pl.multiple_of(row * det_own, det_own), det_own)
        return (
            remote(ts.at[:, cols], tsb.at[s, there, :], s_ts.at[s, d], r_ts.at[s, d], (t, to)),
            remote(sw.at[:, cols], swb.at[s, there, :], s_sw.at[s, d], r_sw.at[s, d], (t, to)),
        )

    def send_span(s):
        for d in range(1, n_wf):
            for copy in chunk(s, d, False):
                copy.start()

    over_tm(lambda d: map_out(d).start())
    if gather_w:
        over_tm(lambda d: w1_out(d).start())
    early = EARLY if gather_w else spans
    for s in range(early):
        send_span(s)

    resp[...] = jnp.concatenate([resp_in[...], jnp.zeros((5, det), F32)], axis=0).T

    home = [homes[tiles[c, k]] for c in range(spans) for k in range(hits)]
    lane = lax.broadcasted_iota(jnp.int32, (8, part_rows), 1)
    lane_home = jnp.zeros((8, part_rows), jnp.int32)
    for p in range(rows):
        lane_home = jnp.where(lane // 8 == p, home[p], lane_home)
    lane_comp = lane - lane // 8 * 8
    lane_owner = lane_home // tiles_own
    before = jnp.zeros((8, part_rows), jnp.int32)
    for p in range(rows):
        before += jnp.where((lane_owner == home[p] // tiles_own) & (lane // 8 > p), 1, 0)
    lane_row = jnp.where(lane_comp < 3, before * 3 + lane_comp, -1)
    lane_id = (lane_home - lane_owner * tiles_own + lane_comp * tiles_own + 1).astype(F32)
    row8 = lax.broadcasted_iota(jnp.int32, (8, part_rows), 0)
    lanes = idb.shape[2]
    places = []
    for o in range(n_tm):
        for m in range(0, pack, 8):
            place = jnp.where((lane_owner == o) & (lane_row == row8 + m), 1.0, 0.0)
            places.append(place)
            label = jnp.sum(place * lane_id, axis=1, keepdims=True) - 1.0
            ids[o, m : m + 8] = jnp.broadcast_to(label, (8, lanes))
    place = jnp.concatenate(places, axis=0)
    own_ids.start()
    over_tm(lambda d: id_out(d).start())

    at = lax.broadcasted_iota(jnp.int32, (8, all_tiles), 1)
    comp = lax.broadcasted_iota(jnp.int32, (8, all_tiles), 0)
    named = [at == home[p] for p in range(rows)]
    own_map.wait()
    over_tm(lambda d: map_in(d).wait_recv())
    total = jnp.zeros((part_rows, pixels), F32)
    for j in range(3):
        pick = jnp.concatenate([jnp.where(n & (comp == j), 1.0, 0.0) for n in named], axis=0).astype(BF16)
        plane = mapb[:, j * tiles_own : (j + 1) * tiles_own].reshape(all_tiles, pixels)
        total += jnp.dot(pick, plane, preferred_element_type=F32)
    fs[...] = total
    own_point.wait()

    if gather_w:
        own_w.wait()
        over_tm(lambda d: w1_in(d).wait_recv())
        mate = w + 1 - 2 * lax.rem(w, 2)
        far = lax.rem(w + 2, n_wf)
        far_mate = far + 1 - 2 * lax.rem(far, 2)

        def w2(kind, arriving):
            who = (mate, far, mate)[kind]
            block = ((mate, far, far_mate) if arriving else (w, w, far))[kind]
            return remote(wbuf.at[:, block], wbuf.at[:, block], s_w2.at[kind], r_w2.at[kind], (t, who))

        w2(1, False).start()
        w2(0, False).start()
        if not CHAIN:
            for s in range(early, spans):
                send_span(s)

    def signal_of(c, carry):
        acc = jnp.zeros((8, samples), F32)
        for k in range(hits):
            tile = fs[pl.ds(pl.multiple_of((c * hits + k) * 8, 8), 8), :].astype(BF16)
            acc += lax.dot_general(tile, point[c, k], (((1,), (1,)), ((), ())), preferred_element_type=F32)
        sig[c] = acc
        return carry

    lax.fori_loop(0, spans, signal_of, 0)

    if gather_w:
        w2(1, True).wait_recv()
        w2(2, False).start()
        w2(0, True).wait_recv()
        w2(2, True).wait_recv()

    block = 256
    per_block = block * n_tm // det

    def weights_at(i):
        if gather_w:
            return wbuf[pl.ds(i * per_block, per_block)].reshape(block, det)
        return whiten[pl.ds(pl.multiple_of(i * block, block), block), :]

    def one_span(s, carry):
        for copy in own_chunk(s):
            copy.wait()
        for d in range(1, n_wf):
            for copy in chunk(s, d, True):
                copy.wait_recv()
        if gather_w and CHAIN:

            @pl.when(s + early < spans)
            def _():
                send_span(s + early)

        srow = sig[s]

        def first(i, carry):
            here = pl.ds(pl.multiple_of(i * block, block), block)
            r = resp[here, :]
            signal = r[:, 0:1] * srow[0:1] + r[:, 1:2] * srow[1:2] + r[:, 2:3] * srow[2:3]
            err = (tsb[s, here, :].astype(F32) - signal) * swb[s, here, :].astype(F32)
            filt[here, :] = jnp.dot(err.astype(BF16), band[...], preferred_element_type=F32).astype(BF16)
            return carry

        lax.fori_loop(0, det // block, first, 0)

        def second(i, acc):
            here = pl.ds(pl.multiple_of(i * block, block), block)
            white = jnp.dot(weights_at(i), filt[...], preferred_element_type=F32).astype(BF16)
            smooth = lax.dot_general(white, band[...], (((1,), (1,)), ((), ())), preferred_element_type=F32)
            x = smooth.astype(BF16).astype(F32) * swb[s, here, :].astype(F32)
            r = resp[here, :]
            return tuple(a + jnp.sum(x * r[:, j : j + 1], axis=0, keepdims=True) for j, a in enumerate(acc))

        zero = jnp.zeros((1, samples), F32)
        acc = lax.fori_loop(0, det // block, second, (zero, zero, zero))
        stokes = jnp.concatenate([*acc, jnp.zeros((5, samples), F32)], axis=0).astype(BF16)
        for k in range(hits):
            there = pl.ds(pl.multiple_of((s * hits + k) * 8, 8), 8)
            part[there, :] = jnp.dot(stokes, point[s, k], preferred_element_type=F32)
        return carry

    lax.fori_loop(0, spans, one_span, 0)

    outb[...] = jnp.dot(place, part[...], preferred_element_type=F32, precision=lax.Precision.HIGHEST).reshape(
        n_tm, pack, pixels
    )
    own_out = pltpu.make_async_copy(outb.at[t], arrb.at[t], loc.at[2 * spans + 3])
    own_out.start()

    def sum_out(d):
        return remote(outb.at[tm_to(d)], arrb.at[t], s_out.at[d], r_out.at[d], (tm_to(d), w))

    def sum_in(d):
        return remote(outb.at[tm_to(d)], arrb.at[tm_from(d)], s_out.at[d], r_out.at[d], (tm_to(d), w))

    over_tm(lambda d: sum_out(d).start())
    own_ids.wait()
    over_tm(lambda d: id_in(d).wait_recv())
    width = 3 * tiles_own
    spot = lax.broadcasted_iota(jnp.int32, (n_tm * pack, lanes), 1).astype(F32)
    hit = jnp.where(idb[...].reshape(n_tm * pack, lanes) == spot, 1.0, 0.0)
    own_out.wait()
    over_tm(lambda d: sum_in(d).wait_recv())
    owned = lax.dot_general(
        hit,
        arrb[...].reshape(n_tm * pack, pixels),
        (((0,), (0,)), ((), ())),
        preferred_element_type=F32,
        precision=lax.Precision.HIGHEST,
    )
    sums[w] = owned[:width]

    def share(d, arriving):
        to = lax.rem(w + d, n_wf)
        slot = lax.rem(w + n_wf - d, n_wf) if arriving else w
        return remote(sums.at[w], sums.at[slot], s_sum.at[d], r_sum.at[d], (t, to))

    for d in range(1, n_wf):
        share(d, False).start()
    for d in range(1, n_wf):
        share(d, True).wait_recv()
    result = sums[0]
    for i in range(1, n_wf):
        result = result + sums[i]
    result = result * float(det) ** (-0.5)
    out_res[...] = result
    out_way[...] = result + scal[1] * way[...]

    def sent(d):
        map_out(d).wait_send()
        id_out(d).wait_send()
        if gather_w:
            w1_out(d).wait_send()
        sum_out(d).wait_send()

    over_tm(sent)
    for d in range(1, n_wf):
        share(d, False).wait_send()

    def spans_sent(s, carry):
        for d in range(1, n_wf):
            for copy in chunk(s, d, False):
                copy.wait_send()
        return carry

    lax.fori_loop(0, spans, spans_sent, 0)
    if gather_w:
        for kind in range(3):
            w2(kind, False).wait_send()


def shards(
    timestream,
    sample_weight,
    response,
    band_filter,
    whiten,
    group_wafer,
    pointing,
    tile_list,
    tile_home,
    solution,
    direction,
    cg_scalars,
):
    n_tm = lax.axis_size("tm")
    n_wf = lax.axis_size("wafer")
    tiles_own, comps, pixels = solution.shape
    spans, hits = tile_list.shape
    samples = band_filter.shape[0]
    w_rows, det = whiten.shape[1:]
    rows = spans * hits
    cap = max(2, (rows + n_tm - 1) // n_tm)
    pack = (3 * cap + 7) // 8 * 8
    lanes = (3 * tiles_own + 127) // 128 * 128
    gather_w = w_rows % 16 == 0 and n_wf == 4 and 256 * n_tm % det == 0
    if not gather_w:
        wsel = sum(jnp.where((group_wafer == v)[:, None, None], whiten[v][None], 0) for v in range(whiten.shape[0]))
        mine = lax.all_to_all(wsel, "tm", split_axis=0, concat_axis=0, tiled=True)
        whiten = lax.all_gather(mine, "wafer", axis=1, tiled=True).reshape(det, det)

    any_space = pl.BlockSpec(memory_space=pl.ANY)
    vmem = pl.BlockSpec(memory_space=pltpu.VMEM)
    dma = pltpu.SemaphoreType.DMA
    dims = (n_tm, n_wf, det, spans, hits, samples, pixels, tiles_own, pack, gather_w)
    part_rows = rows * 8
    w_shape = (n_tm, n_wf, w_rows, det) if gather_w else (1, 1, 16, 128)
    smem = pl.BlockSpec(memory_space=pltpu.SMEM)
    plane = jax.ShapeDtypeStruct((3 * tiles_own, pixels), F32)
    results = pl.pallas_call(
        functools.partial(body, dims),
        out_shape=[plane] * 3,
        in_specs=[any_space, any_space, vmem, smem, any_space, vmem, vmem, vmem, vmem, smem, smem, smem],
        out_specs=[vmem] * 3,
        scratch_shapes=[
            pltpu.VMEM((spans, det, samples), BF16),
            pltpu.VMEM((spans, det, samples), BF16),
            pltpu.VMEM((n_tm, w_rows, det) if gather_w else (1, 16, 128), BF16),
            pltpu.VMEM(w_shape, BF16),
            pltpu.VMEM(pointing.shape, BF16),
            pltpu.VMEM((n_tm, 3 * tiles_own, pixels), BF16),
            pltpu.VMEM((n_tm, pack, lanes), F32),
            pltpu.VMEM((part_rows, pixels), F32),
            pltpu.VMEM((spans, 8, samples), F32),
            pltpu.VMEM((det, samples), BF16),
            pltpu.VMEM((part_rows, pixels), F32),
            pltpu.VMEM((n_tm, pack, pixels), F32),
            pltpu.VMEM((n_tm, pack, pixels), F32),
            pltpu.VMEM((n_wf, 3 * tiles_own, pixels), F32),
            pltpu.VMEM((3 * tiles_own, pixels), BF16),
            pltpu.VMEM((n_tm, pack, lanes), F32),
            pltpu.VMEM((det, 8), F32),
            dma((2 * spans + 5,)),
            dma((spans, n_wf)),
            dma((spans, n_wf)),
            dma((spans, n_wf)),
            dma((spans, n_wf)),
            dma((n_tm,)),
            dma((n_tm,)),
            dma((3,)),
            dma((3,)),
            dma((n_tm,)),
            dma((n_tm,)),
            dma((n_tm,)),
            dma((n_tm,)),
            dma((n_tm,)),
            dma((n_tm,)),
            dma((n_wf,)),
            dma((n_wf,)),
        ],
        compiler_params=pltpu.CompilerParams(
            collective_id=0, has_side_effects=True, vmem_limit_bytes=56 * 1024 * 1024
        ),
    )(
        timestream,
        sample_weight,
        whiten,
        group_wafer,
        pointing,
        band_filter,
        response,
        solution.transpose(1, 0, 2).reshape(3 * tiles_own, pixels),
        direction.transpose(1, 0, 2).reshape(3 * tiles_own, pixels),
        cg_scalars,
        tile_list,
        tile_home,
    )
    return tuple(x.reshape(3, tiles_own, pixels).transpose(1, 0, 2) for x in results)


def solution(mesh):
    in_specs = (
        P("wafer", "tm"),
        P("wafer", "tm"),
        P(),
        P(),
        P(None, ("tm", "wafer"), None),
        P(),
        P(("tm", "wafer"), None, None, None),
        P(("tm", "wafer"), None),
        P(),
        P("tm", None, None),
        P("tm", None, None),
        P(),
    )
    out_specs = (P("tm", None, None), P("tm", None, None), P("tm", None, None))
    return jax.shard_map(shards, mesh=mesh, in_specs=in_specs, out_specs=out_specs, check_vma=False)
```
